32 devices in a mesh: aa: 4 (over x, core), ba: 8 (over z, y).
Axes of the slice: x: 2, y: 2, z: 4, core: 2. Of those that a mesh axis runs over, the one named last changes fastest.
Arguments:
- coefficients: float32 [3072, 3072], P('aa', 'ba'), may hold values from -6 to 6
- tile_values: bfloat16 [4, 3, 768, 768], P('aa'), may hold values from -0.125 to 0.125
- tile_cols: int32 [4, 3], P('aa'), may hold values from 0 to 3, as said below
- alpha_energy: float32 [3072], P('aa'), may hold values from -1 to 1
- beta_energy: float32 [3072], P('ba'), may hold values from -1 to 1
Outputs:
- sigma: float32 [3072, 3072], P('aa', 'ba')
The draws below stay inside these ranges and needn't reach their ends.
Inputs may be any that keep to these rules, and one draw needn't show every extreme that they name: Row r of tile_cols holds r - 1, r and r + 1 taken modulo 4, each once, in some order.
All inputs are finite; a program needn't handle non-finite values.
Results may differ from the reference program's by a relative error of at most 0.0027.
Values may be sent and summed in bfloat16 or wider, within the bound.
A program may use at most 64 MiB of HBM per device.

```python
from functools import partial
import jax
import jax.numpy as jnp
from jax import lax

TILE = 768
SLOTS = 3
NBLK = 4
NSTR = 3072


def draw_tile_cols(key, part):
    rows_ids = jnp.arange(NBLK, dtype=jnp.int32)
    scores = jax.random.randint(key, (NBLK, 3), 0, 1000, dtype=jnp.int32) * 3 + jnp.arange(3, dtype=jnp.int32)[None, :]
    order = jnp.argsort(scores, axis=1, stable=True).astype(jnp.int32)
    offsets = order - 1
    return ((rows_ids[:, None] + offsets + NBLK) % NBLK).astype(jnp.int32)


def block_levels(stream_key, extent, split, least, top_value):
    loudness, own = 1.0, jax.random.fold_in(stream_key, 6)
    for position, shards_of in split:
        steps = jnp.exp(jax.random.uniform(jax.random.fold_in(own, position), (shards_of,), jnp.float32, least / len(split), top_value / len(split)))
        loudness = loudness * jnp.repeat(steps, extent[position] // shards_of).reshape([-1 if axis == position else 1 for axis in range(len(extent))])
    return loudness


def centred(stream_key, shape, scale, limit, pieces=(), held_as=jnp.bfloat16):
    entries = jax.random.normal(stream_key, shape, jnp.float32) * scale
    if len(pieces) > 0:
        entries = block_levels(stream_key, shape, pieces, -0.22, 0.18) * entries
    return jnp.clip(entries, min=-limit, max=limit).astype(held_as)


def setup_inputs(seed: int = 0) -> dict:
    arg_keys = jax.random.split(jax.random.key(seed), 6)
    return {
        "coefficients": centred(arg_keys[0], (NSTR, NSTR), 1.0, 6.0, ((0, 4), (1, 8)), jnp.float32),
        "tile_values": centred(arg_keys[1], (NBLK, SLOTS, TILE, TILE), (3 * TILE) ** -0.5, 0.125, ((0, 4),)),
        "tile_cols": draw_tile_cols(jax.random.fold_in(arg_keys[5], 71), 0),
        "alpha_energy": jnp.clip(jax.random.uniform(arg_keys[3], (NSTR,), jnp.float32, -1.0, 1.0) * block_levels(arg_keys[3], (NSTR,), ((0, 4),), -0.4, 0.0), -1.0, 1.0),
        "beta_energy": jnp.clip(jax.random.uniform(arg_keys[4], (NSTR,), jnp.float32, -1.0, 1.0) * block_levels(arg_keys[4], (NSTR,), ((0, 8),), -0.4, 0.0), -1.0, 1.0),
    }


def block_rows(source, entry):
    tile_group, col_ids = entry
    summed = jnp.zeros((TILE, NSTR), jnp.float32)
    for slot in range(SLOTS):
        picked = lax.dynamic_index_in_dim(source, col_ids[slot].astype(jnp.int32), 0, keepdims=False)
        summed = summed + jnp.dot(tile_group[slot].astype(jnp.float32), picked, precision=lax.Precision.HIGHEST)
    return summed


def reference(coefficients, tile_values, tile_cols, alpha_energy, beta_energy):
    coeff_low = coefficients.astype(jnp.bfloat16).astype(jnp.float32)
    blocks = coeff_low.reshape(NBLK, TILE, NSTR)
    alpha_term = lax.map(partial(block_rows, blocks), (tile_values, tile_cols)).reshape(NSTR, NSTR)
    flipped = coeff_low.T.reshape(NBLK, TILE, NSTR)
    beta_flip = lax.map(partial(block_rows, flipped), (tile_values, tile_cols)).reshape(NSTR, NSTR)
    energy = alpha_energy[:, None] + beta_energy[None, :]
    return alpha_term + beta_flip.T + energy * coefficients
```

```python
import functools

import jax
import jax.numpy as jnp
from jax import lax
from jax.experimental import pallas as pl
from jax.experimental.pallas import tpu as pltpu
from jax.sharding import PartitionSpec as P

MESH = pl.DeviceIdType.MESH


def kernel(count, c_ref, h_hbm, cols_ref, ae_ref, be_ref, out_ref,
           ha, hb, c16, nb, g, rs, rr, own,
           load_sem, y_send, y_recv, z_send, z_recv, a_send, a_recv,
           h_send, h_recv, w_send, f_send, r_send, r_recv):
    a = lax.axis_index("aa")
    b = lax.axis_index("ba")
    side = b % 2
    core = a % 2
    block = b // 2
    partner = b + 1 - 2 * side
    sibling = a + 1 - 2 * core
    blocks = 2 * count
    rows, width = c_ref.shape
    half = rows // 2
    quarter = rows // 4
    up_a, down_a = (a + 1) % count, (a + count - 1) % count
    up_b, down_b = (b + 2) % blocks, (b + blocks - 2) % blocks

    loads = [pltpu.make_async_copy(h_hbm.at[0, s], ha.at[s], load_sem.at[s]) for s in range(3)]
    for load in loads:
        load.start()

    barrier = pltpu.get_barrier_semaphore()
    greeted = [((a + d) % count, b) for d in range(1, count)]
    greeted += [(a, partner), (a, up_b), (a, down_b)]
    for device in greeted:
        pl.semaphore_signal(barrier, inc=1, device_id=device, device_id_type=MESH)

    c16[...] = c_ref[...].astype(jnp.bfloat16)
    g[1, side] = c16[pl.ds(pl.multiple_of(side * half, half), half), :]

    def remote(src, dst, send, recv, device):
        return pltpu.make_async_remote_copy(
            src_ref=src, dst_ref=dst, send_sem=send, recv_sem=recv,
            device_id=device, device_id_type=MESH)

    y_copy = remote(c16.at[pl.ds(pl.multiple_of((1 - side) * half, half), half)],
                    g.at[1, side], y_send.at[0], y_recv.at[0], (a, partner))
    y_wait = remote(g.at[1, 1 - side], g.at[1, 1 - side], y_send.at[0], y_recv.at[0], (a, partner))

    def z_copies(which, column):
        return [remote(g.at[1, column], g.at[0, column], z_send.at[0, which], z_recv.at[0, which], (a, up_b)),
                remote(g.at[1, column], g.at[2, column], z_send.at[1, which], z_recv.at[1, which], (a, down_b))]

    a_copies = [remote(c16, nb.at[0], a_send.at[0], a_recv.at[0], (up_a, b)),
                remote(c16, nb.at[1], a_send.at[1], a_recv.at[1], (down_a, b))]

    pl.semaphore_wait(barrier, len(greeted))
    y_copy.start()
    z_own = z_copies(0, side)
    for copy in z_own:
        copy.start()

    for load in loads:
        load.wait()
    found = [cols_ref[0, s] for s in range(3)]

    def slot_of(offset):
        target = (a + offset + count) % count
        return jnp.where(found[0] == target, 0, jnp.where(found[1] == target, 1, 2))

    slots = [slot_of(offset) for offset in (-1, 0, 1)]

    def piece(s, q):
        return hb.at[s, pl.ds(pl.multiple_of(q * quarter, quarter), quarter)]

    source = a == block
    near = a // 2 == block // 2
    pairs = count // 2

    def spread(s, d, c):
        pair = (a // 2 + d) % pairs
        q = 2 * side + c
        return remote(piece(s, q), piece(s, q), h_send.at[s, d - 1, c], h_recv.at[s, q], (2 * pair + c, b))

    def whole(s):
        return remote(hb.at[s], hb.at[s], w_send.at[s], h_recv.at[s, 0], (sibling, b))

    def forward(s, q, device, index):
        return remote(piece(s, q), piece(s, q), f_send.at[s, index], h_recv.at[s, q], device)

    @pl.when(source)
    def _():
        for s in range(3):
            @pl.loop(0, 4)
            def _(i):
                at = pl.ds(pl.multiple_of(i * quarter, quarter), quarter)
                hb[s, at, :] = ha[slots[s], at, :]
            for d in range(1, pairs):
                for c in range(2):
                    spread(s, d, c).start()
            whole(s).start()

    y_wait.wait_recv()
    z_far = z_copies(1, 1 - side)
    for copy in z_far:
        copy.start()
    for copy in a_copies:
        copy.start()

    tile = rows // 3

    @pl.loop(0, 3)
    def _(i):
        at = pl.ds(pl.multiple_of(i * tile, tile), tile)
        column = jnp.transpose(jnp.broadcast_to(ae_ref[0:1, at], (128, tile)))[:, 0:1]
        energy = column + be_ref[...]
        out_ref[at, :] = energy * c_ref[at, :] + jnp.dot(
            ha[slots[1], at, :], c16[...], preferred_element_type=jnp.float32)

    mine, theirs = 2 * side + core, 2 * (1 - side) + core

    @pl.when(jnp.logical_not(near))
    def _():
        for s in range(3):
            forward(s, mine, (a, partner), 0).wait_recv()
            forward(s, mine, (a, partner), 0).start()
            forward(s, mine, (sibling, b), 1).start()
        for s in range(3):
            forward(s, theirs, (sibling, b), 2).wait_recv()
            forward(s, theirs, (sibling, b), 2).start()
        for s in range(3):
            forward(s, 2 * side + 1 - core, (sibling, b), 1).wait_recv()
            forward(s, 2 * (1 - side) + 1 - core, (sibling, b), 1).wait_recv()

    @pl.when(jnp.logical_and(near, jnp.logical_not(source)))
    def _():
        for s in range(3):
            whole(s).wait_recv()

    for copy in z_own + z_far:
        copy.wait_recv()

    def beta(j, start, size):
        at = pl.ds(pl.multiple_of(start, 128), size)
        total = None
        for k in (1, 0, 2):
            left = jnp.concatenate([g[k, 0], g[k, 1]], axis=1)
            product = lax.dot_general(left, hb[k, at, :], (((1,), (1,)), ((), ())),
                                      preferred_element_type=jnp.float32)
            total = product if total is None else total + product
        return total

    rs[...] = beta(0, (1 - side) * width, width).astype(jnp.bfloat16)
    r_copy = remote(rs, rr, r_send.at[0], r_recv.at[0], (a, partner))
    r_copy.start()
    at_own = pl.ds(pl.multiple_of(side * half, half), half)
    at_other = pl.ds(pl.multiple_of((1 - side) * half, half), half)
    out_ref[at_own, :] += beta(0, side * width, width)

    for copy in a_copies:
        copy.wait_recv()

    @pl.loop(0, 3)
    def _(i):
        at = pl.ds(pl.multiple_of(i * tile, tile), tile)
        out_ref[at, :] += jnp.dot(
            ha[slots[0], at, :], nb[0], preferred_element_type=jnp.float32
        ) + jnp.dot(ha[slots[2], at, :], nb[1], preferred_element_type=jnp.float32)

    r_copy.wait_recv()
    out_ref[at_other, :] += rr[...].astype(jnp.float32)

    for copy in z_own + z_far + a_copies + [y_copy, r_copy]:
        copy.wait_send()

    @pl.when(source)
    def _():
        for s in range(3):
            for d in range(1, pairs):
                for c in range(2):
                    spread(s, d, c).wait_send()
            whole(s).wait_send()

    @pl.when(jnp.logical_not(near))
    def _():
        for s in range(3):
            forward(s, mine, (a, partner), 0).wait_send()
            forward(s, mine, (sibling, b), 1).wait_send()
            forward(s, theirs, (sibling, b), 2).wait_send()


def body(count, coefficients, tile_values, tile_cols, alpha_energy, beta_energy):
    rows, width = coefficients.shape
    half = rows // 2
    low = jnp.bfloat16
    dma = pltpu.SemaphoreType.DMA
    vmem = pl.BlockSpec(memory_space=pltpu.VMEM)
    return pl.pallas_call(
        functools.partial(kernel, count),
        out_shape=jax.ShapeDtypeStruct((rows, width), jnp.float32),
        in_specs=[vmem, pl.BlockSpec(memory_space=pl.ANY),
                  pl.BlockSpec(memory_space=pltpu.SMEM), vmem, vmem],
        out_specs=vmem,
        scratch_shapes=[
            pltpu.VMEM((3, rows, rows), low),
            pltpu.VMEM((3, rows, rows), low),
            pltpu.VMEM((rows, width), low),
            pltpu.VMEM((2, rows, width), low),
            pltpu.VMEM((3, 2, half, width), low),
            pltpu.VMEM((half, width), low),
            pltpu.VMEM((half, width), low),
            pltpu.VMEM((8, 128), jnp.float32),
            dma((3,)), dma((1,)), dma((1,)), dma((2, 2)), dma((2, 2)), dma((2,)), dma((2,)),
            dma((3, count // 2 - 1, 2)), dma((3, 4)), dma((3,)), dma((3, 3)), dma((1,)), dma((1,)),
        ],
        compiler_params=pltpu.CompilerParams(
            collective_id=0, has_side_effects=True, vmem_limit_bytes=48 * 1024 * 1024),
        cost_estimate=pl.CostEstimate(
            flops=12 * rows * rows * width, bytes_accessed=8 * rows * rows, transcendentals=0),
    )(coefficients, tile_values, tile_cols,
      alpha_energy.reshape(1, rows), beta_energy.reshape(1, width))


def solution(mesh):
    in_specs = (P("aa", "ba"), P("aa", None, None, None), P("aa", None), P("aa"), P("ba"))
    return jax.shard_map(functools.partial(body, mesh.shape["aa"]), mesh=mesh,
                         in_specs=in_specs, out_specs=P("aa", "ba"), check_vma=False)
```

```python
import functools

import jax
import jax.numpy as jnp
from jax import lax
from jax.experimental import pallas as pl
from jax.experimental.pallas import tpu as pltpu
from jax.sharding import PartitionSpec as P

MESH = pl.DeviceIdType.MESH


def kernel(count, c_hbm, h_hbm, cols_hbm, ae_ref, be_ref, out_ref,
           c_ref, cols_ref, ha, hb, c16, nb, g, rs, rr,
           load_sem, y_send, y_recv, z_send, z_recv, a_send, a_recv,
           h_send, h_recv, w_send, f_send, r_send, r_recv):
    a = lax.axis_index("aa")
    b = lax.axis_index("ba")
    side = b % 2
    core = a % 2
    block = b // 2
    partner = b + 1 - 2 * side
    sibling = a + 1 - 2 * core
    blocks = 2 * count
    rows, width = c_ref.shape
    half = rows // 2
    quarter = rows // 4
    up_a, down_a = (a + 1) % count, (a + count - 1) % count
    up_b, down_b = (b + 2) % blocks, (b + blocks - 2) % blocks

    first = pltpu.make_async_copy(c_hbm, c_ref, load_sem.at[3])
    first.start()
    loads = [pltpu.make_async_copy(h_hbm.at[0, s], ha.at[s], load_sem.at[s]) for s in range(3)]
    loads.append(pltpu.make_async_copy(cols_hbm, cols_ref, load_sem.at[4]))
    for load in loads:
        load.start()

    barrier = pltpu.get_barrier_semaphore()
    greeted = [((a + d) % count, b) for d in range(1, count)]
    greeted += [(a, partner), (a, up_b), (a, down_b)]
    for device in greeted:
        pl.semaphore_signal(barrier, inc=1, device_id=device, device_id_type=MESH)

    first.wait()
    c16[...] = c_ref[...].astype(jnp.bfloat16)
    g[1, side] = c16[pl.ds(pl.multiple_of(side * half, half), half), :]

    def remote(src, dst, send, recv, device):
        return pltpu.make_async_remote_copy(
            src_ref=src, dst_ref=dst, send_sem=send, recv_sem=recv,
            device_id=device, device_id_type=MESH)

    y_copy = remote(c16.at[pl.ds(pl.multiple_of((1 - side) * half, half), half)],
                    g.at[1, side], y_send.at[0], y_recv.at[0], (a, partner))
    y_wait = remote(g.at[1, 1 - side], g.at[1, 1 - side], y_send.at[0], y_recv.at[0], (a, partner))

    def z_copies(which, column):
        return [remote(g.at[1, column], g.at[0, column], z_send.at[0, which], z_recv.at[0, which], (a, up_b)),
                remote(g.at[1, column], g.at[2, column], z_send.at[1, which], z_recv.at[1, which], (a, down_b))]

    a_copies = [remote(c16, nb.at[0], a_send.at[0], a_recv.at[0], (up_a, b)),
                remote(c16, nb.at[1], a_send.at[1], a_recv.at[1], (down_a, b))]

    def start_cross():
        @pl.when(core == 1)
        def _():
            a_copies[0].start()

        @pl.when(core == 0)
        def _():
            a_copies[1].start()

    pl.semaphore_wait(barrier, len(greeted))
    y_copy.start()
    z_own = z_copies(0, side)
    for copy in z_own:
        copy.start()

    @pl.when(core == 0)
    def _():
        a_copies[0].start()

    @pl.when(core == 1)
    def _():
        a_copies[1].start()

    for load in loads:
        load.wait()
    found = [cols_ref[0, s] for s in range(3)]

    def slot_of(offset):
        target = (a + offset + count) % count
        return jnp.where(found[0] == target, 0, jnp.where(found[1] == target, 1, 2))

    slots = [slot_of(offset) for offset in (-1, 0, 1)]

    def piece(s, q):
        return hb.at[s, pl.ds(pl.multiple_of(q * quarter, quarter), quarter)]

    source = a == block
    near = a // 2 == block // 2
    pairs = count // 2

    def spread(s, d, c):
        pair = (a // 2 + d) % pairs
        q = 2 * (1 - side) + c
        return remote(piece(s, q), piece(s, q), h_send.at[s, d - 1, c], h_recv.at[s, q], (2 * pair + c, b))

    def whole(s):
        return remote(hb.at[s], hb.at[s], w_send.at[s], h_recv.at[s, 0], (sibling, b))

    def forward(s, q, device, index):
        return remote(piece(s, q), piece(s, q), f_send.at[s, index], h_recv.at[s, q], device)

    @pl.when(source)
    def _():
        for s in range(3):
            @pl.loop(0, 4)
            def _(i):
                at = pl.ds(pl.multiple_of(i * quarter, quarter), quarter)
                hb[s, at, :] = ha[slots[s], at, :]
            for d in range(1, pairs):
                for c in range(2):
                    spread(s, d, c).start()
            whole(s).start()

    y_wait.wait_recv()
    z_far = z_copies(1, 1 - side)
    for copy in z_far:
        copy.start()
    @pl.when(jnp.logical_not(near))
    def _():
        start_cross()

    tile = rows // 3

    @pl.loop(0, 3)
    def _(i):
        at = pl.ds(pl.multiple_of(i * tile, tile), tile)
        column = jnp.transpose(jnp.broadcast_to(ae_ref[0:1, at], (128, tile)))[:, 0:1]
        energy = column + be_ref[...]
        out_ref[at, :] = energy * c_ref[at, :] + jnp.dot(
            ha[slots[1], at, :], c16[...], preferred_element_type=jnp.float32)

    mine, theirs = 2 * (1 - side) + core, 2 * side + core

    @pl.when(jnp.logical_not(near))
    def _():
        for s in range(3):
            forward(s, mine, (a, partner), 0).wait_recv()
            forward(s, mine, (a, partner), 0).start()
            forward(s, mine, (sibling, b), 1).start()
        for s in range(3):
            forward(s, theirs, (sibling, b), 2).wait_recv()
            forward(s, theirs, (sibling, b), 2).start()
        for s in range(3):
            forward(s, 2 * (1 - side) + 1 - core, (sibling, b), 1).wait_recv()
            forward(s, 2 * side + 1 - core, (sibling, b), 1).wait_recv()

    @pl.when(jnp.logical_and(near, jnp.logical_not(source)))
    def _():
        for s in range(3):
            whole(s).wait_recv()

    for copy in z_own:
        copy.wait_recv()

    @pl.when(source)
    def _():
        for s in range(3):
            for d in range(1, pairs):
                for c in range(2):
                    spread(s, d, c).wait_send()

    @pl.when(near)
    def _():
        start_cross()

    for copy in z_far:
        copy.wait_recv()

    def beta(j, start, size):
        at = pl.ds(pl.multiple_of(start, 128), size)
        total = None
        for k in (1, 0, 2):
            left = jnp.concatenate([g[k, 0], g[k, 1]], axis=1)
            product = lax.dot_general(left, hb[k, at, :], (((1,), (1,)), ((), ())),
                                      preferred_element_type=jnp.float32)
            total = product if total is None else total + product
        return total

    rs[...] = beta(0, (1 - side) * width, width).astype(jnp.bfloat16)
    r_copy = remote(rs, rr, r_send.at[0], r_recv.at[0], (a, partner))
    r_copy.start()
    at_own = pl.ds(pl.multiple_of(side * half, half), half)
    at_other = pl.ds(pl.multiple_of((1 - side) * half, half), half)
    out_ref[at_own, :] += beta(0, side * width, width)

    for copy in a_copies:
        copy.wait_recv()

    @pl.loop(0, 3)
    def _(i):
        at = pl.ds(pl.multiple_of(i * tile, tile), tile)
        out_ref[at, :] += jnp.dot(
            ha[slots[0], at, :], nb[0], preferred_element_type=jnp.float32
        ) + jnp.dot(ha[slots[2], at, :], nb[1], preferred_element_type=jnp.float32)

    r_copy.wait_recv()
    out_ref[at_other, :] += rr[...].astype(jnp.float32)

    for copy in z_own + z_far + a_copies + [y_copy, r_copy]:
        copy.wait_send()

    @pl.when(source)
    def _():
        for s in range(3):
            whole(s).wait_send()

    @pl.when(jnp.logical_not(near))
    def _():
        for s in range(3):
            forward(s, mine, (a, partner), 0).wait_send()
            forward(s, mine, (sibling, b), 1).wait_send()
            forward(s, theirs, (sibling, b), 2).wait_send()


def body(count, coefficients, tile_values, tile_cols, alpha_energy, beta_energy):
    rows, width = coefficients.shape
    half = rows // 2
    low = jnp.bfloat16
    dma = pltpu.SemaphoreType.DMA
    hbm = pl.BlockSpec(memory_space=pltpu.HBM)
    vmem = pl.BlockSpec(memory_space=pltpu.VMEM)
    return pl.pallas_call(
        functools.partial(kernel, count),
        out_shape=jax.ShapeDtypeStruct((rows, width), jnp.float32),
        in_specs=[hbm, hbm, hbm, vmem, vmem],
        out_specs=vmem,
        scratch_shapes=[
            pltpu.VMEM((rows, width), jnp.float32),
            pltpu.SMEM(tile_cols.shape, jnp.int32),
            pltpu.VMEM((3, rows, rows), low),
            pltpu.VMEM((3, rows, rows), low),
            pltpu.VMEM((rows, width), low),
            pltpu.VMEM((2, rows, width), low),
            pltpu.VMEM((3, 2, half, width), low),
            pltpu.VMEM((half, width), low),
            pltpu.VMEM((half, width), low),
            dma((5,)), dma((1,)), dma((1,)), dma((2, 2)), dma((2, 2)), dma((2,)), dma((2,)),
            dma((3, count // 2 - 1, 2)), dma((3, 4)), dma((3,)), dma((3, 3)), dma((1,)), dma((1,)),
        ],
        compiler_params=pltpu.CompilerParams(
            collective_id=0, has_side_effects=True, vmem_limit_bytes=63 * 1024 * 1024),
        cost_estimate=pl.CostEstimate(
            flops=12 * rows * rows * width, bytes_accessed=8 * rows * rows, transcendentals=0),
    )(coefficients, tile_values, tile_cols,
      alpha_energy.reshape(1, rows), beta_energy.reshape(1, width))


def solution(mesh):
    in_specs = (P("aa", "ba"), P("aa", None, None, None), P("aa", None), P("aa"), P("ba"))
    return jax.shard_map(functools.partial(body, mesh.shape["aa"]), mesh=mesh,
                         in_specs=in_specs, out_specs=P("aa", "ba"), check_vma=False)
```

```python
import functools

import jax
import jax.numpy as jnp
from jax import lax
from jax.experimental import pallas as pl
from jax.experimental.pallas import tpu as pltpu
from jax.sharding import PartitionSpec as P

MESH = pl.DeviceIdType.MESH


def kernel(count, c_hbm, h_hbm, cols_hbm, out_ref,
           c_ref, cols_ref, ha, hb, c16, nb, g, rs, rr,
           load_sem, y_send, y_recv, z_send, z_recv, a_send, a_recv,
           h_send, h_recv, w_send, f_send, r_send, r_recv):
    a = lax.axis_index("aa")
    b = lax.axis_index("ba")
    side = b % 2
    core = a % 2
    block = b // 2
    partner = b + 1 - 2 * side
    sibling = a + 1 - 2 * core
    blocks = 2 * count
    rows, width = c_ref.shape
    half = rows // 2
    quarter = rows // 4
    up_a, down_a = (a + 1) % count, (a + count - 1) % count
    up_b, down_b = (b + 2) % blocks, (b + blocks - 2) % blocks

    first = pltpu.make_async_copy(c_hbm, c_ref, load_sem.at[3])
    first.start()
    loads = [pltpu.make_async_copy(h_hbm.at[0, s], ha.at[s], load_sem.at[s]) for s in range(3)]
    loads.append(pltpu.make_async_copy(cols_hbm, cols_ref, load_sem.at[4]))
    for load in loads:
        load.start()

    barrier = pltpu.get_barrier_semaphore()
    greeted = [((a + d) % count, b) for d in range(1, count)]
    greeted += [(a, partner), (a, up_b), (a, down_b)]
    for device in greeted:
        pl.semaphore_signal(barrier, inc=1, device_id=device, device_id_type=MESH)

    first.wait()
    c16[...] = c_ref[...].astype(jnp.bfloat16)
    g[1, side] = c16[pl.ds(pl.multiple_of(side * half, half), half), :]

    def remote(src, dst, send, recv, device):
        return pltpu.make_async_remote_copy(
            src_ref=src, dst_ref=dst, send_sem=send, recv_sem=recv,
            device_id=device, device_id_type=MESH)

    y_copy = remote(c16.at[pl.ds(pl.multiple_of((1 - side) * half, half), half)],
                    g.at[1, side], y_send.at[0], y_recv.at[0], (a, partner))
    y_wait = remote(g.at[1, 1 - side], g.at[1, 1 - side], y_send.at[0], y_recv.at[0], (a, partner))

    def z_copies(which, column):
        return [remote(g.at[1, column], g.at[0, column], z_send.at[0, which], z_recv.at[0, which], (a, up_b)),
                remote(g.at[1, column], g.at[2, column], z_send.at[1, which], z_recv.at[1, which], (a, down_b))]

    a_copies = [remote(c16, nb.at[0], a_send.at[0], a_recv.at[0], (up_a, b)),
                remote(c16, nb.at[1], a_send.at[1], a_recv.at[1], (down_a, b))]

    def start_cross():
        @pl.when(core == 1)
        def _():
            a_copies[0].start()

        @pl.when(core == 0)
        def _():
            a_copies[1].start()

    pl.semaphore_wait(barrier, len(greeted))
    y_copy.start()
    z_own = z_copies(0, side)
    for copy in z_own:
        copy.start()

    @pl.when(core == 0)
    def _():
        a_copies[0].start()

    @pl.when(core == 1)
    def _():
        a_copies[1].start()

    for load in loads:
        load.wait()
    found = [cols_ref[0, s] for s in range(3)]

    def slot_of(offset):
        target = (a + offset + count) % count
        return jnp.where(found[0] == target, 0, jnp.where(found[1] == target, 1, 2))

    slots = [slot_of(offset) for offset in (-1, 0, 1)]

    def piece(s, q):
        return hb.at[s, pl.ds(pl.multiple_of(q * quarter, quarter), quarter)]

    source = a == block
    near = a // 2 == block // 2
    pairs = count // 2

    def spread(s, d, c):
        pair = (a // 2 + d) % pairs
        q = 2 * (1 - side) + c
        return remote(piece(s, q), piece(s, q), h_send.at[s, d - 1, c], h_recv.at[s, q], (2 * pair + c, b))

    def whole(s):
        return remote(hb.at[s], hb.at[s], w_send.at[s], h_recv.at[s, 0], (sibling, b))

    def forward(s, q, device, index):
        return remote(piece(s, q), piece(s, q), f_send.at[s, index], h_recv.at[s, q], device)

    @pl.when(source)
    def _():
        for s in range(3):
            @pl.loop(0, 4)
            def _(i):
                at = pl.ds(pl.multiple_of(i * quarter, quarter), quarter)
                hb[s, at, :] = ha[slots[s], at, :]
            for d in range(1, pairs):
                for c in range(2):
                    spread(s, d, c).start()
            whole(s).start()

    y_wait.wait_recv()
    z_far = z_copies(1, 1 - side)
    for copy in z_far:
        copy.start()
    @pl.when(jnp.logical_not(near))
    def _():
        start_cross()

    mine, theirs = 2 * (1 - side) + core, 2 * side + core

    @pl.when(jnp.logical_not(near))
    def _():
        for s in range(3):
            forward(s, mine, (a, partner), 0).wait_recv()
            forward(s, mine, (a, partner), 0).start()
            forward(s, mine, (sibling, b), 1).start()
        for s in range(3):
            forward(s, theirs, (sibling, b), 2).wait_recv()
            forward(s, theirs, (sibling, b), 2).start()
        for s in range(3):
            forward(s, 2 * (1 - side) + 1 - core, (sibling, b), 1).wait_recv()
            forward(s, 2 * side + 1 - core, (sibling, b), 1).wait_recv()

    @pl.when(jnp.logical_and(near, jnp.logical_not(source)))
    def _():
        for s in range(3):
            whole(s).wait_recv()

    for copy in z_own:
        copy.wait_recv()

    @pl.when(source)
    def _():
        for s in range(3):
            for d in range(1, pairs):
                for c in range(2):
                    spread(s, d, c).wait_send()

    @pl.when(near)
    def _():
        start_cross()

    for copy in z_far:
        copy.wait_recv()

    def beta(j, start, size):
        at = pl.ds(pl.multiple_of(start, 128), size)
        total = None
        for k in (1, 0, 2):
            left = jnp.concatenate([g[k, 0], g[k, 1]], axis=1)
            product = lax.dot_general(left, hb[k, at, :], (((1,), (1,)), ((), ())),
                                      preferred_element_type=jnp.float32)
            total = product if total is None else total + product
        return total

    rs[...] = beta(0, (1 - side) * width, width).astype(jnp.bfloat16)
    r_copy = remote(rs, rr, r_send.at[0], r_recv.at[0], (a, partner))
    r_copy.start()
    at_own = pl.ds(pl.multiple_of(side * half, half), half)
    at_other = pl.ds(pl.multiple_of((1 - side) * half, half), half)
    out_ref[at_other, :] = jnp.zeros((half, width), jnp.float32)
    out_ref[at_own, :] = beta(0, side * width, width)

    for copy in a_copies:
        copy.wait_recv()

    tile = rows // 3

    @pl.loop(0, 3)
    def _(i):
        at = pl.ds(pl.multiple_of(i * tile, tile), tile)
        out_ref[at, :] += jnp.dot(
            ha[slots[1], at, :], c16[...], preferred_element_type=jnp.float32
        ) + jnp.dot(
            ha[slots[0], at, :], nb[0], preferred_element_type=jnp.float32
        ) + jnp.dot(ha[slots[2], at, :], nb[1], preferred_element_type=jnp.float32)

    r_copy.wait_recv()
    out_ref[at_other, :] += rr[...].astype(jnp.float32)

    for copy in z_own + z_far + a_copies + [y_copy, r_copy]:
        copy.wait_send()

    @pl.when(source)
    def _():
        for s in range(3):
            whole(s).wait_send()

    @pl.when(jnp.logical_not(near))
    def _():
        for s in range(3):
            forward(s, mine, (a, partner), 0).wait_send()
            forward(s, mine, (sibling, b), 1).wait_send()
            forward(s, theirs, (sibling, b), 2).wait_send()


def body(count, coefficients, tile_values, tile_cols, alpha_energy, beta_energy):
    rows, width = coefficients.shape
    half = rows // 2
    low = jnp.bfloat16
    dma = pltpu.SemaphoreType.DMA
    hbm = pl.BlockSpec(memory_space=pltpu.HBM)
    vmem = pl.BlockSpec(memory_space=pltpu.VMEM)
    coupled = pl.pallas_call(
        functools.partial(kernel, count),
        out_shape=jax.ShapeDtypeStruct((rows, width), jnp.float32),
        in_specs=[hbm, hbm, hbm],
        out_specs=vmem,
        scratch_shapes=[
            pltpu.VMEM((rows, width), jnp.float32),
            pltpu.SMEM(tile_cols.shape, jnp.int32),
            pltpu.VMEM((3, rows, rows), low),
            pltpu.VMEM((3, rows, rows), low),
            pltpu.VMEM((rows, width), low),
            pltpu.VMEM((2, rows, width), low),
            pltpu.VMEM((3, 2, half, width), low),
            pltpu.VMEM((half, width), low),
            pltpu.VMEM((half, width), low),
            dma((5,)), dma((1,)), dma((1,)), dma((2, 2)), dma((2, 2)), dma((2,)), dma((2,)),
            dma((3, count // 2 - 1, 2)), dma((3, 4)), dma((3,)), dma((3, 3)), dma((1,)), dma((1,)),
        ],
        compiler_params=pltpu.CompilerParams(
            collective_id=0, has_side_effects=True, vmem_limit_bytes=63 * 1024 * 1024),
        cost_estimate=pl.CostEstimate(
            flops=12 * rows * rows * width, bytes_accessed=8 * rows * rows, transcendentals=0),
    )(coefficients, tile_values, tile_cols)
    return coupled + (alpha_energy[:, None] + beta_energy[None, :]) * coefficients


def solution(mesh):
    in_specs = (P("aa", "ba"), P("aa", None, None, None), P("aa", None), P("aa"), P("ba"))
    return jax.shard_map(functools.partial(body, mesh.shape["aa"]), mesh=mesh,
                         in_specs=in_specs, out_specs=P("aa", "ba"), check_vma=False)
```

```python
import functools

import jax
import jax.numpy as jnp
from jax import lax
from jax.experimental import pallas as pl
from jax.experimental.pallas import tpu as pltpu
from jax.sharding import PartitionSpec as P

MESH = pl.DeviceIdType.MESH


def kernel(count, c_hbm, h_hbm, cols_hbm, out_ref,
           c_ref, cols_ref, ha, hb, c16, nb, g, rs, rr,
           load_sem, y_send, y_recv, z_send, z_recv, a_send, a_recv,
           h_send, h_recv, w_send, f_send, r_send, r_recv):
    a = lax.axis_index("aa")
    b = lax.axis_index("ba")
    side = b % 2
    core = a % 2
    block = b // 2
    partner = b + 1 - 2 * side
    sibling = a + 1 - 2 * core
    blocks = 2 * count
    rows, width = c_ref.shape
    half = rows // 2
    quarter = rows // 4
    up_a, down_a = (a + 1) % count, (a + count - 1) % count
    up_b, down_b = (b + 2) % blocks, (b + blocks - 2) % blocks

    first = pltpu.make_async_copy(c_hbm, c_ref, load_sem.at[3])
    first.start()
    loads = [pltpu.make_async_copy(h_hbm.at[0, s], ha.at[s], load_sem.at[s]) for s in range(3)]
    loads.append(pltpu.make_async_copy(cols_hbm, cols_ref, load_sem.at[4]))
    for load in loads:
        load.start()

    barrier = pltpu.get_barrier_semaphore()
    greeted = [((a + d) % count, b) for d in range(1, count)]
    greeted += [(a, partner), (a, up_b), (a, down_b)]
    for device in greeted:
        pl.semaphore_signal(barrier, inc=1, device_id=device, device_id_type=MESH)

    first.wait()
    c16[...] = c_ref[...].astype(jnp.bfloat16)
    g[1, side] = c16[pl.ds(pl.multiple_of(side * half, half), half), :]

    def remote(src, dst, send, recv, device):
        return pltpu.make_async_remote_copy(
            src_ref=src, dst_ref=dst, send_sem=send, recv_sem=recv,
            device_id=device, device_id_type=MESH)

    y_copy = remote(c16.at[pl.ds(pl.multiple_of((1 - side) * half, half), half)],
                    g.at[1, side], y_send.at[0], y_recv.at[0], (a, partner))
    y_wait = remote(g.at[1, 1 - side], g.at[1, 1 - side], y_send.at[0], y_recv.at[0], (a, partner))

    def z_copies(which, column):
        return [remote(g.at[1, column], g.at[0, column], z_send.at[0, which], z_recv.at[0, which], (a, up_b)),
                remote(g.at[1, column], g.at[2, column], z_send.at[1, which], z_recv.at[1, which], (a, down_b))]

    a_copies = [remote(c16, nb.at[0], a_send.at[0], a_recv.at[0], (up_a, b)),
                remote(c16, nb.at[1], a_send.at[1], a_recv.at[1], (down_a, b))]

    def start_cross():
        @pl.when(core == 1)
        def _():
            a_copies[0].start()

        @pl.when(core == 0)
        def _():
            a_copies[1].start()

    pl.semaphore_wait(barrier, len(greeted))
    y_copy.start()
    z_own = z_copies(0, side)
    for copy in z_own:
        copy.start()

    @pl.when(core == 0)
    def _():
        a_copies[0].start()

    @pl.when(core == 1)
    def _():
        a_copies[1].start()

    for load in loads:
        load.wait()
    found = [cols_ref[0, s] for s in range(3)]

    def slot_of(offset):
        target = (a + offset + count) % count
        return jnp.where(found[0] == target, 0, jnp.where(found[1] == target, 1, 2))

    slots = [slot_of(offset) for offset in (-1, 0, 1)]

    def piece(s, q):
        return hb.at[s, pl.ds(pl.multiple_of(q * quarter, quarter), quarter)]

    source = a == block
    near = a // 2 == block // 2
    pairs = count // 2

    def spread(s, d, c):
        pair = (a // 2 + d) % pairs
        q = 2 * (1 - side) + c
        return remote(piece(s, q), piece(s, q), h_send.at[s, d - 1, c], h_recv.at[s, q], (2 * pair + c, b))

    def whole(s):
        return remote(hb.at[s], hb.at[s], w_send.at[s], h_recv.at[s, 0], (sibling, b))

    def forward(s, q, device, index):
        return remote(piece(s, q), piece(s, q), f_send.at[s, index], h_recv.at[s, q], device)

    @pl.when(source)
    def _():
        for s in range(3):
            @pl.loop(0, 4)
            def _(i):
                at = pl.ds(pl.multiple_of(i * quarter, quarter), quarter)
                hb[s, at, :] = ha[slots[s], at, :]
            if s == 0:
                for d in range(1, pairs):
                    for c in range(2):
                        spread(s, d, c).start()
            whole(s).start()

    y_wait.wait_recv()
    z_far = z_copies(1, 1 - side)
    for copy in z_far:
        copy.start()
    @pl.when(jnp.logical_not(near))
    def _():
        start_cross()

    @pl.when(source)
    def _():
        for s in range(1, 3):
            for d in range(1, pairs):
                for c in range(2):
                    spread(s - 1, d, c).wait_send()
                    spread(s, d, c).start()

    mine, theirs = 2 * (1 - side) + core, 2 * side + core

    @pl.when(jnp.logical_not(near))
    def _():
        for s in range(3):
            forward(s, mine, (a, partner), 0).wait_recv()
            forward(s, mine, (a, partner), 0).start()
            forward(s, mine, (sibling, b), 1).start()
        for s in range(3):
            forward(s, theirs, (sibling, b), 2).wait_recv()
            forward(s, theirs, (sibling, b), 2).start()
        for s in range(3):
            forward(s, 2 * (1 - side) + 1 - core, (sibling, b), 1).wait_recv()
            forward(s, 2 * side + 1 - core, (sibling, b), 1).wait_recv()

    @pl.when(jnp.logical_and(near, jnp.logical_not(source)))
    def _():
        for s in range(3):
            whole(s).wait_recv()

    for copy in z_own:
        copy.wait_recv()

    @pl.when(source)
    def _():
        for d in range(1, pairs):
            for c in range(2):
                spread(2, d, c).wait_send()

    @pl.when(near)
    def _():
        start_cross()

    for copy in z_far:
        copy.wait_recv()

    def beta(j, start, size):
        at = pl.ds(pl.multiple_of(start, 128), size)
        total = None
        for k in (1, 0, 2):
            left = jnp.concatenate([g[k, 0], g[k, 1]], axis=1)
            product = lax.dot_general(left, hb[k, at, :], (((1,), (1,)), ((), ())),
                                      preferred_element_type=jnp.float32)
            total = product if total is None else total + product
        return total

    rs[...] = beta(0, (1 - side) * width, width).astype(jnp.bfloat16)
    r_copy = remote(rs, rr, r_send.at[0], r_recv.at[0], (a, partner))
    r_copy.start()
    at_own = pl.ds(pl.multiple_of(side * half, half), half)
    at_other = pl.ds(pl.multiple_of((1 - side) * half, half), half)
    out_ref[at_other, :] = jnp.zeros((half, width), jnp.float32)
    out_ref[at_own, :] = beta(0, side * width, width)

    for copy in a_copies:
        copy.wait_recv()

    tile = rows // 3

    @pl.loop(0, 3)
    def _(i):
        at = pl.ds(pl.multiple_of(i * tile, tile), tile)
        out_ref[at, :] += jnp.dot(
            ha[slots[1], at, :], c16[...], preferred_element_type=jnp.float32
        ) + jnp.dot(
            ha[slots[0], at, :], nb[0], preferred_element_type=jnp.float32
        ) + jnp.dot(ha[slots[2], at, :], nb[1], preferred_element_type=jnp.float32)

    r_copy.wait_recv()
    out_ref[at_other, :] += rr[...].astype(jnp.float32)

    for copy in z_own + z_far + a_copies + [y_copy, r_copy]:
        copy.wait_send()

    @pl.when(source)
    def _():
        for s in range(3):
            whole(s).wait_send()

    @pl.when(jnp.logical_not(near))
    def _():
        for s in range(3):
            forward(s, mine, (a, partner), 0).wait_send()
            forward(s, mine, (sibling, b), 1).wait_send()
            forward(s, theirs, (sibling, b), 2).wait_send()


def body(count, coefficients, tile_values, tile_cols, alpha_energy, beta_energy):
    rows, width = coefficients.shape
    half = rows // 2
    low = jnp.bfloat16
    dma = pltpu.SemaphoreType.DMA
    hbm = pl.BlockSpec(memory_space=pltpu.HBM)
    vmem = pl.BlockSpec(memory_space=pltpu.VMEM)
    coupled = pl.pallas_call(
        functools.partial(kernel, count),
        out_shape=jax.ShapeDtypeStruct((rows, width), jnp.float32),
        in_specs=[hbm, hbm, hbm],
        out_specs=vmem,
        scratch_shapes=[
            pltpu.VMEM((rows, width), jnp.float32),
            pltpu.SMEM(tile_cols.shape, jnp.int32),
            pltpu.VMEM((3, rows, rows), low),
            pltpu.VMEM((3, rows, rows), low),
            pltpu.VMEM((rows, width), low),
            pltpu.VMEM((2, rows, width), low),
            pltpu.VMEM((3, 2, half, width), low),
            pltpu.VMEM((half, width), low),
            pltpu.VMEM((half, width), low),
            dma((5,)), dma((1,)), dma((1,)), dma((2, 2)), dma((2, 2)), dma((2,)), dma((2,)),
            dma((3, count // 2 - 1, 2)), dma((3, 4)), dma((3,)), dma((3, 3)), dma((1,)), dma((1,)),
        ],
        compiler_params=pltpu.CompilerParams(
            collective_id=0, has_side_effects=True, vmem_limit_bytes=63 * 1024 * 1024),
        cost_estimate=pl.CostEstimate(
            flops=12 * rows * rows * width, bytes_accessed=8 * rows * rows, transcendentals=0),
    )(coefficients, tile_values, tile_cols)
    return coupled + (alpha_energy[:, None] + beta_energy[None, :]) * coefficients


def solution(mesh):
    in_specs = (P("aa", "ba"), P("aa", None, None, None), P("aa", None), P("aa"), P("ba"))
    return jax.shard_map(functools.partial(body, mesh.shape["aa"]), mesh=mesh,
                         in_specs=in_specs, out_specs=P("aa", "ba"), check_vma=False)
```

```python
import functools

import jax
import jax.numpy as jnp
from jax import lax
from jax.experimental import pallas as pl
from jax.experimental.pallas import tpu as pltpu
from jax.sharding import PartitionSpec as P

MESH = pl.DeviceIdType.MESH


def kernel(count, c_hbm, h_hbm, cols_hbm, out_ref,
           c_ref, cols_ref, ha, hb, c16, nb, g, rs, rr,
           load_sem, y_send, y_recv, z_send, z_recv, a_send, a_recv,
           h_send, h_recv, w_send, f_send, r_send, r_recv):
    a = lax.axis_index("aa")
    b = lax.axis_index("ba")
    side = b % 2
    core = a % 2
    block = b // 2
    partner = b + 1 - 2 * side
    sibling = a + 1 - 2 * core
    blocks = 2 * count
    rows, width = c_ref.shape
    half = rows // 2
    quarter = rows // 4
    up_a, down_a = (a + 1) % count, (a + count - 1) % count
    up_b, down_b = (b + 2) % blocks, (b + blocks - 2) % blocks

    first = pltpu.make_async_copy(c_hbm, c_ref, load_sem.at[3])
    first.start()
    loads = [pltpu.make_async_copy(h_hbm.at[0, s], ha.at[s], load_sem.at[s]) for s in range(3)]
    loads.append(pltpu.make_async_copy(cols_hbm, cols_ref, load_sem.at[4]))
    for load in loads:
        load.start()

    barrier = pltpu.get_barrier_semaphore()
    greeted = [((a + d) % count, b) for d in range(1, count)]
    greeted += [(a, partner), (a, up_b), (a, down_b)]
    for device in greeted:
        pl.semaphore_signal(barrier, inc=1, device_id=device, device_id_type=MESH)

    first.wait()
    c16[...] = c_ref[...].astype(jnp.bfloat16)
    g[1, side] = c16[pl.ds(pl.multiple_of(side * half, half), half), :]

    def remote(src, dst, send, recv, device):
        return pltpu.make_async_remote_copy(
            src_ref=src, dst_ref=dst, send_sem=send, recv_sem=recv,
            device_id=device, device_id_type=MESH)

    y_copy = remote(c16.at[pl.ds(pl.multiple_of((1 - side) * half, half), half)],
                    g.at[1, side], y_send.at[0], y_recv.at[0], (a, partner))
    y_wait = remote(g.at[1, 1 - side], g.at[1, 1 - side], y_send.at[0], y_recv.at[0], (a, partner))

    def z_copies(which, column):
        return [remote(g.at[1, column], g.at[0, column], z_send.at[0, which], z_recv.at[0, which], (a, up_b)),
                remote(g.at[1, column], g.at[2, column], z_send.at[1, which], z_recv.at[1, which], (a, down_b))]

    a_copies = [remote(c16, nb.at[0], a_send.at[0], a_recv.at[0], (up_a, b)),
                remote(c16, nb.at[1], a_send.at[1], a_recv.at[1], (down_a, b))]

    def start_cross():
        @pl.when(core == 1)
        def _():
            a_copies[0].start()

        @pl.when(core == 0)
        def _():
            a_copies[1].start()

    pl.semaphore_wait(barrier, len(greeted))
    y_copy.start()
    z_own = z_copies(0, side)
    for copy in z_own:
        copy.start()

    @pl.when(core == 0)
    def _():
        a_copies[0].start()

    @pl.when(core == 1)
    def _():
        a_copies[1].start()

    for load in loads:
        load.wait()
    found = [cols_ref[0, s] for s in range(3)]

    def slot_of(offset):
        target = (a + offset + count) % count
        return jnp.where(found[0] == target, 0, jnp.where(found[1] == target, 1, 2))

    slots = [slot_of(offset) for offset in (-1, 0, 1)]

    def piece(s, q):
        return hb.at[s, pl.ds(pl.multiple_of(q * quarter, quarter), quarter)]

    source = a == block
    near = a // 2 == block // 2
    pairs = count // 2

    def spread(s, d, c):
        pair = (a // 2 + d) % pairs
        q = 2 * (1 - side) + c
        return remote(piece(s, q), piece(s, q), h_send.at[s, d - 1, c], h_recv.at[s, q], (2 * pair + c, b))

    def whole(s):
        return remote(hb.at[s], hb.at[s], w_send.at[s], h_recv.at[s, 0], (sibling, b))

    def forward(s, q, device, index):
        return remote(piece(s, q), piece(s, q), f_send.at[s, index], h_recv.at[s, q], device)

    @pl.when(source)
    def _():
        for s in range(3):
            @pl.loop(0, 4)
            def _(i):
                at = pl.ds(pl.multiple_of(i * quarter, quarter), quarter)
                hb[s, at, :] = ha[slots[s], at, :]
            for d in range(1, pairs):
                for c in range(2):
                    spread(s, d, c).start()
            whole(s).start()

    y_wait.wait_recv()
    z_far = z_copies(1, 1 - side)
    for copy in z_far:
        copy.start()
    @pl.when(jnp.logical_not(source))
    def _():
        start_cross()

    mine, theirs = 2 * (1 - side) + core, 2 * side + core

    @pl.when(jnp.logical_not(near))
    def _():
        for s in range(3):
            forward(s, mine, (a, partner), 0).wait_recv()
            forward(s, mine, (a, partner), 0).start()
            forward(s, mine, (sibling, b), 1).start()
        for s in range(3):
            forward(s, theirs, (sibling, b), 2).wait_recv()
            forward(s, theirs, (sibling, b), 2).start()
        for s in range(3):
            forward(s, 2 * (1 - side) + 1 - core, (sibling, b), 1).wait_recv()
            forward(s, 2 * side + 1 - core, (sibling, b), 1).wait_recv()

    @pl.when(jnp.logical_and(near, jnp.logical_not(source)))
    def _():
        for s in range(3):
            whole(s).wait_recv()

    for copy in z_own:
        copy.wait_recv()

    @pl.when(source)
    def _():
        for s in range(3):
            for d in range(1, pairs):
                for c in range(2):
                    spread(s, d, c).wait_send()

    @pl.when(source)
    def _():
        start_cross()

    for copy in z_far:
        copy.wait_recv()

    def beta(j, start, size):
        at = pl.ds(pl.multiple_of(start, 128), size)
        total = None
        for k in (1, 0, 2):
            left = jnp.concatenate([g[k, 0], g[k, 1]], axis=1)
            product = lax.dot_general(left, hb[k, at, :], (((1,), (1,)), ((), ())),
                                      preferred_element_type=jnp.float32)
            total = product if total is None else total + product
        return total

    rs[...] = beta(0, (1 - side) * width, width).astype(jnp.bfloat16)
    r_copy = remote(rs, rr, r_send.at[0], r_recv.at[0], (a, partner))
    r_copy.start()
    at_own = pl.ds(pl.multiple_of(side * half, half), half)
    at_other = pl.ds(pl.multiple_of((1 - side) * half, half), half)
    out_ref[at_other, :] = jnp.zeros((half, width), jnp.float32)
    out_ref[at_own, :] = beta(0, side * width, width)

    for copy in a_copies:
        copy.wait_recv()

    tile = rows // 3

    @pl.loop(0, 3)
    def _(i):
        at = pl.ds(pl.multiple_of(i * tile, tile), tile)
        out_ref[at, :] += jnp.dot(
            ha[slots[1], at, :], c16[...], preferred_element_type=jnp.float32
        ) + jnp.dot(
            ha[slots[0], at, :], nb[0], preferred_element_type=jnp.float32
        ) + jnp.dot(ha[slots[2], at, :], nb[1], preferred_element_type=jnp.float32)

    r_copy.wait_recv()
    out_ref[at_other, :] += rr[...].astype(jnp.float32)

    for copy in z_own + z_far + a_copies + [y_copy, r_copy]:
        copy.wait_send()

    @pl.when(source)
    def _():
        for s in range(3):
            whole(s).wait_send()

    @pl.when(jnp.logical_not(near))
    def _():
        for s in range(3):
            forward(s, mine, (a, partner), 0).wait_send()
            forward(s, mine, (sibling, b), 1).wait_send()
            forward(s, theirs, (sibling, b), 2).wait_send()


def body(count, coefficients, tile_values, tile_cols, alpha_energy, beta_energy):
    rows, width = coefficients.shape
    half = rows // 2
    low = jnp.bfloat16
    dma = pltpu.SemaphoreType.DMA
    hbm = pl.BlockSpec(memory_space=pltpu.HBM)
    vmem = pl.BlockSpec(memory_space=pltpu.VMEM)
    coupled = pl.pallas_call(
        functools.partial(kernel, count),
        out_shape=jax.ShapeDtypeStruct((rows, width), jnp.float32),
        in_specs=[hbm, hbm, hbm],
        out_specs=vmem,
        scratch_shapes=[
            pltpu.VMEM((rows, width), jnp.float32),
            pltpu.SMEM(tile_cols.shape, jnp.int32),
            pltpu.VMEM((3, rows, rows), low),
            pltpu.VMEM((3, rows, rows), low),
            pltpu.VMEM((rows, width), low),
            pltpu.VMEM((2, rows, width), low),
            pltpu.VMEM((3, 2, half, width), low),
            pltpu.VMEM((half, width), low),
            pltpu.VMEM((half, width), low),
            dma((5,)), dma((1,)), dma((1,)), dma((2, 2)), dma((2, 2)), dma((2,)), dma((2,)),
            dma((3, count // 2 - 1, 2)), dma((3, 4)), dma((3,)), dma((3, 3)), dma((1,)), dma((1,)),
        ],
        compiler_params=pltpu.CompilerParams(
            collective_id=0, has_side_effects=True, vmem_limit_bytes=63 * 1024 * 1024),
        cost_estimate=pl.CostEstimate(
            flops=12 * rows * rows * width, bytes_accessed=8 * rows * rows, transcendentals=0),
    )(coefficients, tile_values, tile_cols)
    return coupled + (alpha_energy[:, None] + beta_energy[None, :]) * coefficients


def solution(mesh):
    in_specs = (P("aa", "ba"), P("aa", None, None, None), P("aa", None), P("aa"), P("ba"))
    return jax.shard_map(functools.partial(body, mesh.shape["aa"]), mesh=mesh,
                         in_specs=in_specs, out_specs=P("aa", "ba"), check_vma=False)
```
